128 devices in a mesh: lon: 16 (over y, z), lat: 4 (over x_lo, core), lev: 2 (over x_hi).
Axes of the slice: x: 4 (x_hi: 2, x_lo: 2; x = x_hi * 2 + x_lo), y: 4, z: 4, core: 2. Of those that a mesh axis runs over, the one named last changes fastest.
Arguments:
- tracers: float32 [4, 6, 1800, 2048], P(None, 'lev', 'lat', 'lon'), parts along dimension 1, may hold values from -6 to 6
- zonal_courant: float32 [6, 1800, 2048], P('lev', 'lat', 'lon'), parts along dimension 0, as said below
- merid_courant: float32 [6, 1800, 2048], P('lev', 'lat', 'lon'), parts along dimension 0, may hold values from -0.25 to 0.25
Outputs:
- advected: float32 [4, 6, 1800, 2048], P(None, 'lev', 'lat', 'lon'), parts along dimension 1
The draws below stay inside these ranges and needn't reach their ends.
There are 2 independent parts, one for each index of `lev`. The reference program is written for one: setup_inputs(seed, part) draws one part's arguments, and reference() takes and returns one part's arrays. A program takes and returns all parts, laid end to end along the dimension named above; each array names one. Nothing has to cross between parts.
Inputs may be any that keep to these rules, and one draw needn't show every extreme that they name: `zonal_courant`: magnitudes are at most 0.25 outside the first 224 and last 224 rows of the globe and at most 1 inside them.
All inputs are finite; a program needn't handle non-finite values.
Results may differ from the reference program's by a relative error of at most 0.0003.
Values sent between devices are 32-bit elements; how exact they have to be, the bound alone decides.
No kernel may reach another device: no remote copies, remote signals or barrier semaphores. Data moves between devices by JAX's collectives and lax.ppermute only.
A program may use at most 128 MiB of HBM per device.

```python
import jax
import jax.numpy as jnp
from jax import lax

F = 4
L = 3
NSUB = 4
NSTEPS = 3
PCAP = 224
NLAT = 1800
NLON = 2048


def draw_zonal_courant(key, part):
    key = jax.random.fold_in(key, 7)
    spread = jax.random.uniform(key, (L, NLAT, NLON), jnp.float32, -1.0, 1.0)
    row_index = jnp.arange(NLAT)
    in_cap = (row_index < PCAP) | (row_index >= NLAT - PCAP)
    amplitude = jnp.where(in_cap, 0.25 * NSUB, 0.25).astype(jnp.float32)[:, None]
    return (amplitude * spread).astype(jnp.float32)


def level_of(key, extent, split, least, largest):
    factor_of, own = 1.0, jax.random.fold_in(key, 6)
    for axis_at, shards_of in split:
        steps = jnp.exp(jax.random.uniform(jax.random.fold_in(own, axis_at), (shards_of,), jnp.float32, least / len(split), largest / len(split)))
        factor_of = factor_of * jnp.repeat(steps, extent[axis_at] // shards_of).reshape([-1 if axis == axis_at else 1 for axis in range(len(extent))])
    return factor_of


def bell_draw(own_key, dims, scale, most, shards=(), kind=jnp.bfloat16):
    loudness = level_of(own_key, dims, shards, -0.22, 0.18) if shards else 1.0
    entries = jax.random.normal(own_key, dims, jnp.float32) * scale * loudness
    return jnp.minimum(jnp.maximum(entries, -most), most).astype(kind)


def setup_inputs(seed: int = 0, part: int = 0) -> dict:
    arg_keys = jax.random.split(jax.random.key(seed), 4)
    part_keys = jax.random.split(jax.random.fold_in(arg_keys[3], part), 4)
    return {
        "tracers": bell_draw(part_keys[0], (F, L, NLAT, NLON), 1.0, 6.0, ((2, 4), (3, 16)), jnp.float32),
        "zonal_courant": draw_zonal_courant(jax.random.fold_in(jax.random.fold_in(arg_keys[3], part), 71), part),
        "merid_courant": jnp.clip(jax.random.uniform(part_keys[2], (L, NLAT, NLON), jnp.float32, -0.25, 0.25) * level_of(part_keys[2], (L, NLAT, NLON), ((1, 4), (2, 16)), -0.4, 0.0), -0.25, 0.25),
    }


def face_flux(extended, courant, axis):
    count = extended.shape[axis] - 3
    first = lax.slice_in_dim(extended, 0, count, axis=axis)
    second = lax.slice_in_dim(extended, 1, count + 1, axis=axis)
    third = lax.slice_in_dim(extended, 2, count + 2, axis=axis)
    fourth = lax.slice_in_dim(extended, 3, count + 3, axis=axis)
    rising = (-first + 5.0 * second + 2.0 * third) / 6.0
    falling = (2.0 * second + 5.0 * third - fourth) / 6.0
    return jnp.where(courant > 0, courant * rising, courant * falling)


def zonal_sweep(extended, faces):
    last_axis = extended.ndim - 1
    flux = face_flux(extended, faces, last_axis)
    inner = lax.slice_in_dim(extended, 2, extended.shape[-1] - 2, axis=last_axis)
    return inner - (flux[..., 1:] - flux[..., :-1])


def periodic(field):
    return jnp.concatenate([field[..., -2:], field, field[..., :2]], axis=-1)


def faces_of(courant):
    return jnp.concatenate([courant, courant[..., :1]], axis=-1)


def one_cycle(fields, zonal, merid):
    swept = zonal_sweep(periodic(fields), faces_of(zonal))
    top_faces = faces_of(zonal[:PCAP] / NSUB)
    bottom_faces = faces_of(zonal[NLAT - PCAP:] / NSUB)
    top_rows = fields[:, :PCAP]
    bottom_rows = fields[:, NLAT - PCAP:]
    for substep in range(NSUB):
        top_rows = zonal_sweep(periodic(top_rows), top_faces)
        bottom_rows = zonal_sweep(periodic(bottom_rows), bottom_faces)
    swept = jnp.concatenate([top_rows, swept[:, PCAP:NLAT - PCAP], bottom_rows], axis=1)
    across_top = jnp.roll(swept[:, :1], NLON // 2, axis=-1)
    across_bottom = jnp.roll(swept[:, -1:], NLON // 2, axis=-1)
    empty_row = jnp.zeros_like(across_top)
    padded = jnp.concatenate([empty_row, across_top, swept, across_bottom, empty_row], axis=1)
    merid_faces = jnp.concatenate([merid, jnp.zeros((1, NLON), jnp.float32)], axis=0)
    face_index = jnp.arange(NLAT + 1)
    face_cos = jnp.where((face_index > 0) & (face_index < NLAT),
                         jnp.sin(jnp.pi * face_index.astype(jnp.float32) / NLAT), 0.0)[:, None]
    cell_cos = jnp.sin(jnp.pi * (jnp.arange(NLAT).astype(jnp.float32) + 0.5) / NLAT)[:, None]
    flux = face_flux(padded, merid_faces, 1) * face_cos
    return swept - (flux[:, 1:] - flux[:, :-1]) / cell_cos


def advect_level(inputs):
    fields, zonal, merid = inputs
    for cycle in range(NSTEPS):
        fields = one_cycle(fields, zonal, merid)
    return fields


def reference(tracers, zonal_courant, merid_courant):
    by_level = jnp.moveaxis(tracers, 1, 0)
    result = lax.map(advect_level, (by_level, zonal_courant, merid_courant))
    return jnp.moveaxis(result, 0, 1)
```

```python
import functools

import jax
import jax.numpy as jnp
import numpy as np
from jax import lax
from jax.experimental import pallas as pl
from jax.experimental.pallas import tpu as pltpu
from jax.sharding import PartitionSpec as P

FIELDS, LEVELS = 4, 3
NSUB, NSTEPS, PCAP = 4, 3, 224
BANDS, LOOP = 4, 16
ROWS, LON = 450, 128
GLOBE = ROWS * BANDS
CHUNKS, TILE_STEP = 42, 114
TILES = ((0, 1), (3, 2))
SHIFT_NORTH, SHIFT = 12, 6
E_OWN, E_ROWS = 24, 512
WIDE, NARROW, WIDE_Z, WIDE_M, NARROW_Z, NARROW_M = 24, 6, 23, 16, 5, 4
PAYLOAD = 3 * WIDE + 3 * NARROW + WIDE_Z + WIDE_M + NARROW_Z + NARROW_M
RIM = 24
KEEP, EDGE = 10, 32
INNER_COLS = LON + 16
VMEM_BYTES = 24 * 2**20


def lane_tables():
    band = np.arange(BANDS).reshape(-1, 1, 1, 1, 1)
    tile = np.array(TILES).reshape(1, 2, 1, 2, 1)[:, :, :, np.arange(8) % 2]
    k = np.arange(3).reshape(1, 1, 3, 1, 1)
    chunk = (np.arange(128) % CHUNKS).reshape(1, 1, 1, 1, -1)
    shift = np.where(band == BANDS - 1, SHIFT_NORTH, SHIFT)
    row = band * ROWS + TILE_STEP * tile + 3 * chunk + k - shift
    face = np.where(row % GLOBE == 0, 0.0, np.abs(np.sin(np.pi * row / GLOBE)))
    cell = np.abs(np.sin(np.pi * (row + 0.5) / GLOBE))
    group = np.arange(2).reshape(1, 2, 1, 1, 1)
    polar = (band == 0) & (group == 0) | (band == BANDS - 1) & (group == 1)
    cap = polar & ((row < PCAP) | (row >= GLOBE - PCAP))
    kinds = [face / 6.0, 1.0 / cell, np.where(cap, 1.0 / NSUB, 1.0) / 6.0, cap]
    return np.stack([np.broadcast_to(x, row.shape) for x in kinds], axis=1).astype(np.float32)


def row_payload_kernel(t_hbm, z_hbm, m_hbm, u_ref, v_ref, z_ref, m_ref, rim_ref, sems):
    even = lax.axis_index("lat") % 2 == 0
    last = ROWS * FIELDS - RIM
    copies = [
        pltpu.make_async_copy(z_hbm, z_ref, sems.at[0]),
        pltpu.make_async_copy(m_hbm, m_ref, sems.at[1]),
        pltpu.make_async_copy(t_hbm.at[:, pl.ds(0, RIM), :], rim_ref.at[0], sems.at[2]),
        pltpu.make_async_copy(t_hbm.at[:, pl.ds(last, RIM), :], rim_ref.at[1], sems.at[3]),
    ]
    for copy in copies:
        copy.start()
    for copy in copies:
        copy.wait()

    def put(l, first, south, north):
        u_ref[l, first : first + south.shape[0]] = jnp.where(even, north, south)
        v_ref[l, first : first + south.shape[0]] = jnp.where(even, south, north)

    for l in range(LEVELS):
        put(l, 0, rim_ref[0, l], rim_ref[1, l])
        put(l, RIM, z_ref[l, :8], z_ref[l, ROWS - 8 :])
        put(l, RIM + 8, m_ref[l, :8], m_ref[l, ROWS - 8 :])


def row_payload(tracers, zonal, merid):
    shapes = [(LEVELS, RIM + 16, LON)] * 2 + [(LEVELS, ROWS, LON)] * 2
    return pl.pallas_call(
        row_payload_kernel,
        out_shape=[pltpu.VMEM(shape, jnp.float32) for shape in shapes],
        in_specs=[pl.BlockSpec(memory_space=pltpu.HBM)] * 3,
        out_specs=[pl.BlockSpec(memory_space=pltpu.VMEM)] * len(shapes),
        scratch_shapes=[pltpu.VMEM((2, LEVELS, RIM, LON), jnp.float32), pltpu.SemaphoreType.DMA((4,))],
        compiler_params=pltpu.CompilerParams(vmem_limit_bytes=8 * 2**20),
        name="row_payload",
    )(*[pltpu.with_memory_space_constraint(x, pltpu.HBM) for x in (tracers, zonal, merid)])


def pack_side(side, band, t_ref, e_ref, d_ref, cz_ref, cm_ref):
    base = jnp.where(band == BANDS - 1, E_OWN - SHIFT_NORTH, E_OWN - SHIFT)
    sub = lax.broadcasted_iota(jnp.int32, (8, 128), 0)

    def packed(ref, image, start, per_row):
        x, y, z = (ref[image + l, pl.ds(start - 6 * per_row * l, 48, stride=3 * per_row), :] for l in range(3))
        rows = [x[:40], jnp.where(sub < 2, x[40:], y[:8]), y[8:40], jnp.where(sub < 4, y[40:], z[:8]), z[8:]]
        return jnp.concatenate(rows, axis=0).T

    for g in range(2):
        for k in range(3):
            start = base + TILE_STEP * TILES[g][side] + k
            for f in range(FIELDS):
                d_ref[g * 3 + k, pl.ds(2 * f + side, LON, stride=8), :] = packed(t_ref, 0, start * FIELDS + f, FIELDS)
            cz_ref[g, pl.ds(2 * k + side, LON, stride=8), :] = packed(e_ref, 0, start, 1)
            cm_ref[g, pl.ds(2 * k + side, LON, stride=8), :] = packed(e_ref, LEVELS, start, 1)


def pack_middle_kernel(t_hbm, z_ref, m_ref, after_ref, t_ref, e_ref, d_ref, cz_ref, cm_ref, sems):
    copies = []
    for l in range(LEVELS):
        own = t_ref.at[l, pl.ds(E_OWN * FIELDS, ROWS * FIELDS), :]
        copies.append(pltpu.make_async_copy(t_hbm.at[l], own, sems.at[l]))
        copies[l].start()
    north_end = E_OWN + ROWS
    for l in range(LEVELS):
        t_ref[l, : 4 * E_OWN] = jnp.zeros((4 * E_OWN, LON), jnp.float32)
        t_ref[l, 4 * north_end :] = jnp.zeros((4 * (E_ROWS - north_end), LON), jnp.float32)
        for i, ref in ((l, z_ref), (LEVELS + l, m_ref)):
            e_ref[i, :E_OWN] = jnp.zeros((E_OWN, LON), jnp.float32)
            e_ref[i, E_OWN:north_end] = ref[l]
            e_ref[i, north_end:] = jnp.zeros((E_ROWS - north_end, LON), jnp.float32)
    for copy in copies:
        copy.wait()
    pack_side(1, lax.axis_index("lat"), t_ref, e_ref, d_ref, cz_ref, cm_ref)


ROW_SHAPES = [(LEVELS, E_ROWS * FIELDS, LON), (2 * LEVELS, E_ROWS, LON)]
CELL_SHAPES = [(6, INNER_COLS * 8, 128), (2, (LON + 1) * 8, 128), (2, (LON + 1) * 8, 128)]


def pack_middle(tracers, zonal, merid, after):
    shapes = ROW_SHAPES + CELL_SHAPES
    args = [pltpu.with_memory_space_constraint(tracers, pltpu.HBM)]
    args += [pltpu.with_memory_space_constraint(x, pltpu.VMEM) for x in (zonal, merid, after)]
    return pl.pallas_call(
        pack_middle_kernel,
        out_shape=[pltpu.VMEM(shape, jnp.float32) for shape in shapes],
        in_specs=[pl.BlockSpec(memory_space=pltpu.HBM)] + [pl.BlockSpec(memory_space=pltpu.VMEM)] * 3,
        out_specs=[pl.BlockSpec(memory_space=pltpu.VMEM)] * len(shapes),
        scratch_shapes=[pltpu.SemaphoreType.DMA((LEVELS,))],
        compiler_params=pltpu.CompilerParams(vmem_limit_bytes=8 * 2**20),
        name="pack_middle",
    )(*args)


def pack_rims_kernel(t_in, e_in, d_in, cz_in, cm_in, ru, rv, t_ref, e_ref, d_ref, cz_ref, cm_ref, sw_ref, se_ref):
    band = lax.axis_index("lat")
    even = band % 2 == 0
    north_end = E_OWN + ROWS
    for l in range(LEVELS):
        u, v = ru[l, :RIM], rv[l, :RIM]
        t_ref[l, 4 * E_OWN - RIM : 4 * E_OWN] = jnp.where(even, v, u)
        t_ref[l, 4 * north_end : 4 * north_end + RIM] = jnp.where(even, u, v)
        for i, at in ((l, RIM), (LEVELS + l, RIM + 8)):
            u, v = ru[l, at : at + 8], rv[l, at : at + 8]
            e_ref[i, E_OWN - 8 : E_OWN] = jnp.where(even, v, u)
            e_ref[i, north_end : north_end + 8] = jnp.where(even, u, v)

    def mirrored(start, t_start):
        for l in range(LEVELS):
            for h in range(RIM // 4):
                t_ref[l, t_start + 4 * h : t_start + 4 * (h + 1)] = rv[l, RIM - 4 * (h + 1) : RIM - 4 * h]
            for h in range(8):
                e_ref[l, start + h : start + h + 1] = rv[l, RIM + 7 - h : RIM + 8 - h]
                if h > 0:
                    e_ref[LEVELS + l, start + h : start + h + 1] = -rv[l, RIM + 16 - h : RIM + 17 - h]
                else:
                    e_ref[LEVELS + l, start : start + 1] = jnp.zeros((1, LON), jnp.float32)

    @pl.when(band == 0)
    def _():
        mirrored(E_OWN - 8, 4 * E_OWN - RIM)

    @pl.when(band == BANDS - 1)
    def _():
        mirrored(north_end, 4 * north_end)

    pack_side(0, band, t_ref, e_ref, d_ref, cz_ref, cm_ref)
    wide = jnp.where(band == BANDS - 1, 1, 0)
    thin = 1 - wide

    def payload(out, east):
        at = 0

        def put(ref, index, width):
            nonlocal at
            first = LON - width if east else 0
            out[pl.ds(at * 8, width * 8), :] = ref[index, pl.ds(first * 8, width * 8), :]
            at += width

        for k in range(3):
            put(d_ref, wide * 3 + k, WIDE)
        for k in range(3):
            put(d_ref, thin * 3 + k, NARROW)
        put(cz_ref, wide, WIDE_Z)
        put(cm_ref, wide, WIDE_M)
        put(cz_ref, thin, NARROW_Z)
        put(cm_ref, thin, NARROW_M)

    payload(sw_ref, False)
    payload(se_ref, True)


def pack_rims(middle, ru, rv):
    shapes = ROW_SHAPES + CELL_SHAPES + [(PAYLOAD * 8, 128)] * 2
    return vmem_call(pack_rims_kernel, shapes, [], "pack_rims", {i: i for i in range(5)})(*middle, ru, rv)[2:]


def vmem_call(kernel, shapes, scratch, name, aliases=None):
    vmem = pl.BlockSpec(memory_space=pltpu.VMEM)

    def call(*args):
        return pl.pallas_call(
            kernel,
            out_shape=[pltpu.VMEM(shape, jnp.float32) for shape in shapes],
            in_specs=[vmem] * len(args),
            out_specs=[vmem] * len(shapes),
            scratch_shapes=scratch,
            input_output_aliases=aliases or {},
            compiler_params=pltpu.CompilerParams(vmem_limit_bytes=VMEM_BYTES),
            name=name,
        )(*[pltpu.with_memory_space_constraint(x, pltpu.VMEM) for x in args])

    return call


def upwind(c, a, b, d, e, b3, d3):
    s = b + d
    return c * ((s + s) + jnp.where(c > 0, b3 - a, d3 - e))


def block(ref, index, first, count):
    return ref[index, pl.ds(pl.multiple_of(first * 8, 8), count * 8), :].reshape(count, 8, 128)


def put_block(ref, index, first, value):
    count = value.shape[0]
    ref[index, pl.ds(pl.multiple_of(first * 8, 8), count * 8), :] = value.reshape(count * 8, 128)


def columns(ref, index, first, count):
    return ref.at[index, pl.ds(pl.multiple_of(first * 8, 8), count * 8), :]


def side_one():
    return lax.broadcasted_iota(jnp.int32, (8, 128), 0) % 2 == 1


def roll(x, steps):
    return pltpu.roll(x.reshape(-1, 128), steps, 1).reshape(x.shape)


def spread(source, source_at, out, out_at, scale, first, chunks, masked_at=None, masks=None):
    odd = side_one()

    def body(j, carry):
        for u in range(8):
            i = first + j * 8 + u
            for k in range(3):
                low = source[source_at, pl.ds(i * 8 + 2 * k, 1), :]
                high = source[source_at, pl.ds(i * 8 + 2 * k + 1, 1), :]
                both = jnp.where(odd, jnp.broadcast_to(high, (8, 128)), jnp.broadcast_to(low, (8, 128))) * scale[k]
                put_block(out, out_at + k, i, both[None])
                if masks is not None:
                    put_block(out, masked_at + k, i, (both * masks[k])[None])
        return carry

    lax.fori_loop(0, chunks, body, 0)


def sweeps(s_ref, c_ref, r_ref, count, unroll, zonal=(), meridional=(), inverse=None, band=None, ahead=True):
    def begin(at, c_at, first):
        p = block(s_ref, at, first - 2, 4)
        flux = upwind(block(c_ref, c_at, first, 1)[0], p[0], p[1], p[2], p[3], 3.0 * p[1], 3.0 * p[2])
        return flux[None], p[1:2]

    if band is not None:
        north = band == BANDS - 1
        turn = jnp.where(north, 38, 90)
        chunk = jnp.where(north, CHUNKS - 1, 0)
        k_first = jnp.where(north, 1, 0)
        lane = lax.broadcasted_iota(jnp.int32, (8, 128), 1)
        hit = side_one() & ((lane == chunk) | (lane == chunk + CHUNKS) | (lane == chunk + 2 * CHUNKS))
        hits = [hit & (k_first <= k) & (k <= k_first + 1) for k in range(3)]

    def prepared(n, at, i):
        p = [block(s_ref, at + k, i, unroll) for k in range(3)]
        moves = [roll(p[1], 1), roll(p[2], 1), roll(p[0], 127)]
        if band is not None:
            moves.extend(roll(x, turn) for x in p)
        return [(r_ref, n * 6 + slot, i, value) for slot, value in enumerate(moves)]

    def store(results):
        for ref, where, i, value in results:
            put_block(ref, where, i, value)

    if ahead:
        for n, (at, c_at, first) in enumerate(meridional):
            store(prepared(n, at, first))

    def body(j, carry):
        results, after, begun, moved = [], [], [], []
        for n, (at, c_at, first) in enumerate(meridional):
            i = first + j * unroll
            p = [block(s_ref, at + k, i, unroll) for k in range(3)]
            if ahead:
                moves = [block(r_ref, n * 6 + slot, i, unroll) for slot in range(3 if band is None else 6)]
                store(prepared(n, at, i + unroll))
            else:
                moves = [value for _, _, _, value in prepared(n, at, i)]
            c0, below, twice_below = block(c_ref, c_at, i, unroll), moves[0], moves[1]
            t0 = 3.0 * p[0]
            f0 = upwind(c0, below, twice_below, p[0], p[1], 3.0 * twice_below, t0)
            begun.append((i, p, t0, f0, roll(f0, 127), twice_below, moves[2]))
            moved.extend(moves[3:])
        for (at, c_at, _), (i, (p0, p1, p2), t0, f0, f0_above, p2_below, p0_above) in zip(meridional, begun, strict=True):
            c1, c2 = (block(c_ref, c_at + k, i, unroll) for k in (1, 2))
            t1, t2 = 3.0 * p1, 3.0 * p2
            f1 = upwind(c1, p2_below, p0, p1, p2, t0, t1)
            f2 = upwind(c2, p0, p1, p2, p0_above, t1, t2)
            results.append((s_ref, at, i, p0 - (f1 - f0) * inverse[0]))
            results.append((s_ref, at + 1, i, p1 - (f2 - f1) * inverse[1]))
            results.append((s_ref, at + 2, i, p2 - (f0_above - f2) * inverse[2]))
        for n, (at, c_at, first) in enumerate(zonal):
            i = first + j * unroll
            for k in range(3):
                flux_before, before = carry[n * 3 + k]
                p = jnp.concatenate([before, block(s_ref, at + k, i, unroll + 2)], axis=0)
                c = block(c_ref, c_at + k, i + 1, unroll)
                p3 = 3.0 * p[1 : unroll + 2]
                flux = upwind(c, p[:unroll], p[1 : unroll + 1], p[2 : unroll + 2], p[3:], p3[:-1], p3[1:])
                west = jnp.concatenate([flux_before, flux[:-1]], axis=0)
                value = p[1 : unroll + 1] - (flux - west)
                if band is not None:
                    value = jnp.where(hits[k], moved[n * 3 + k], value)
                results.append((s_ref, at + k, i, value))
                after.append((flux[-1:], p[unroll : unroll + 1]))
        store(results)
        return tuple(after)

    carry = tuple(begin(at + k, c_at + k, first) for at, c_at, first in zonal for k in range(3))
    if count == 1:
        body(0, carry)
    else:
        lax.fori_loop(0, count, body, carry)


ZONAL_WIDE, ZONAL_MASKED, ZONAL_THIN, MERID_WIDE, MERID_THIN, C_SIZE = 0, 3, 6, 9, 12, 15


def spread_all(tab, band, wide, thin, out, base, zonal, merid, spans):
    for g, span, zonal_at, merid_at in ((wide, spans[0], ZONAL_WIDE, MERID_WIDE), (thin, spans[1], ZONAL_THIN, MERID_THIN)):
        scale, weight, cap = ([tab[band, kind, g, k] for k in range(3)] for kind in (2, 0, 3))
        masked = (base + ZONAL_MASKED, cap) if g is wide else ()
        spread(zonal[0], zonal[1] + g, out, base + zonal_at, scale, *span, *masked)
        spread(merid[0], merid[1] + g, out, base + merid_at, weight, *spans[2])


def keep(state_ref, s_ref, cycle, group):
    edge = 8 * cycle
    for k in range(3):
        i = group * 3 + k
        put_block(state_ref, cycle * 6 + i, 0, block(s_ref, i, edge, KEEP))
        put_block(state_ref, cycle * 6 + i, KEEP, block(s_ref, i, LON - edge - KEEP, KEEP))


def inner_kernel(tab, d_ref, cz_ref, cm_ref, s_ref, state_ref, step_ref, c_ref, r_ref):
    band = lax.axis_index("lat")
    is_cap = (band == 0) | (band == BANDS - 1)
    wide = jnp.where(band == BANDS - 1, 1, 0)
    thin = 1 - wide
    at_wide, at_thin = wide * 3, thin * 3
    inverse_wide, inverse_thin = ([tab[band, 1, g, k] for k in range(3)] for g in (wide, thin))
    spread_all(tab, band, wide, thin, c_ref, 0, (cz_ref, 0), (cm_ref, 0), ((0, LON // 8), (8, LON // 8 - 1), (8, LON // 8 - 2)))
    keep(state_ref, s_ref, 0, wide)
    keep(state_ref, s_ref, 0, thin)
    sweeps(s_ref, c_ref, r_ref, LON // 16, 16, [(at_wide, ZONAL_WIDE, 2)])

    for cycle in range(NSTEPS):
        edge = 8 * (cycle + 1)
        kept = LON - 2 * edge

        @pl.when(is_cap)
        def _(cycle=cycle):
            for sub in range(1, NSUB + 1):
                low = 2 * (NSUB * cycle + sub)
                if sub > 1:
                    width = LON - 2 * low
                    unroll = max(n for n in range(8, 31) if width % n == 0)
                    sweeps(s_ref, c_ref, r_ref, width // unroll, unroll, [(at_wide, ZONAL_MASKED, low)])
                if sub < NSUB:
                    for k in range(3):
                        at = (cycle * 3 + sub - 1) * 3 + k
                        put_block(step_ref, at, 0, block(s_ref, at_wide + k, low, 4))
                        put_block(step_ref, at, 4, block(s_ref, at_wide + k, LON - low - 4, 4))

        beside = band if cycle == 0 else None
        sweeps(s_ref, c_ref, r_ref, kept // 16, 16, [(at_thin, ZONAL_THIN, edge)], [(at_wide, MERID_WIDE, edge)], inverse_wide, beside)
        if cycle < NSTEPS - 1:
            keep(state_ref, s_ref, cycle + 1, wide)
            then = [(at_wide, ZONAL_WIDE, edge + 2)]
        else:
            then = []
        sweeps(s_ref, c_ref, r_ref, kept // 16, 16, then, [(at_thin, MERID_THIN, edge)], inverse_thin)
        if cycle < NSTEPS - 1:
            keep(state_ref, s_ref, cycle + 1, thin)


def run_inner(table, cells, cz, cm):
    shapes = [(6, INNER_COLS * 8, 128), (18, 2 * KEEP * 8, 128), (27, 64, 128)]
    scratch = [pltpu.VMEM((n, INNER_COLS * 8, 128), jnp.float32) for n in (C_SIZE, 6)]
    return vmem_call(inner_kernel, shapes, scratch, "inner_columns", {1: 0})(table, cells, cz, cm)


def outer_kernel(tab, cz_ref, cm_ref, rw_ref, re_ref, done_ref, state_ref, step_ref, out_hbm, s_ref, cu_ref, c_ref, w_ref, o_ref, out_sem):
    band = lax.axis_index("lat")
    is_cap = (band == 0) | (band == BANDS - 1)
    wide = jnp.where(band == BANDS - 1, 1, 0)
    thin = 1 - wide
    for g in range(2):
        for kind, own in ((0, cz_ref), (1, cm_ref)):
            put_block(cu_ref, kind * 2 + g, EDGE, block(own, g, 0, EDGE))
            put_block(cu_ref, 4 + kind * 2 + g, 0, block(own, g, LON - EDGE, EDGE))
    for side, recv in ((0, rw_ref), (1, re_ref)):
        at = 0
        plan = [(s_ref, side * 6 + wide * 3 + k, WIDE) for k in range(3)]
        plan += [(s_ref, side * 6 + thin * 3 + k, NARROW) for k in range(3)]
        plan += [(cu_ref, side * 4 + wide, WIDE_Z), (cu_ref, side * 4 + 2 + wide, WIDE_M)]
        plan += [(cu_ref, side * 4 + thin, NARROW_Z), (cu_ref, side * 4 + 2 + thin, NARROW_M)]
        for ref, index, width in plan:
            first = EDGE if side else EDGE - width
            put_block(ref, index, first, recv[at * 8 : (at + width) * 8, :].reshape(width, 8, 128))
            at += width

    def take(cycle, group):
        edge = 8 * cycle
        for k in range(3):
            i = group * 3 + k
            put_block(s_ref, i, EDGE + edge, block(state_ref, cycle * 6 + i, 0, KEEP))
            put_block(s_ref, 6 + i, EDGE - edge - KEEP, block(state_ref, cycle * 6 + i, KEEP, KEEP))

    def places(at, c_at, first):
        return [(side * 6 + at, side * C_SIZE + c_at, first[side]) for side in range(2)]

    def sweep(zonal, meridional=(), inverse=None, beside=None):
        sweeps(s_ref, c_ref, None, 2, 12, zonal, meridional, inverse, beside, ahead=False)

    def first_zonal(cycle):
        low = jnp.where(is_cap, 8 * cycle + 2, 8 * cycle + 8)
        return places(at_wide, ZONAL_WIDE, (EDGE - WIDE + low, EDGE - low))

    at_wide, at_thin = wide * 3, thin * 3
    inverse_wide, inverse_thin = ([tab[band, 1, g, k] for k in range(3)] for g in (wide, thin))
    for side in range(2):
        near = EDGE - WIDE + (0 if side else 8)
        spans = ((EDGE - WIDE, 6 if side else 7), (near, 6), (near, 5))
        spread_all(tab, band, wide, thin, c_ref, side * C_SIZE, (cu_ref, side * 4), (cu_ref, side * 4 + 2), spans)
    take(0, wide)
    take(0, thin)
    sweep(first_zonal(0))

    for cycle in range(NSTEPS):
        edge = 8 * (cycle + 1)
        first = (EDGE - WIDE + edge, EDGE - edge)

        @pl.when(is_cap)
        def _(cycle=cycle):
            for sub in range(1, NSUB + 1):
                low = 2 * (NSUB * cycle + sub)
                if sub > 1:
                    sweep(places(at_wide, ZONAL_MASKED, (EDGE - WIDE + low, EDGE - low)))
                if sub < NSUB:
                    for k in range(3):
                        at = (cycle * 3 + sub - 1) * 3 + k
                        put_block(s_ref, at_wide + k, EDGE + low, block(step_ref, at, 0, 4))
                        put_block(s_ref, 6 + at_wide + k, EDGE - low - 4, block(step_ref, at, 4, 4))

        beside = band if cycle == 0 else None
        sweep(places(at_thin, ZONAL_THIN, first), places(at_wide, MERID_WIDE, first), inverse_wide, beside)
        if cycle < NSTEPS - 1:
            take(cycle + 1, wide)
            then = first_zonal(cycle + 1)
        else:
            then = []
        sweep(then, places(at_thin, MERID_THIN, first), inverse_thin)
        if cycle < NSTEPS - 1:
            take(cycle + 1, thin)

    north = band == BANDS - 1
    shift = jnp.where(north, SHIFT_NORTH, SHIFT)

    def write_rows(tile, act):
        for is_this, shift_here in ((north, SHIFT_NORTH), (jnp.logical_not(north), SHIFT)):
            low = max(0, TILE_STEP * tile + 6 - shift_here)
            high = min(ROWS, TILE_STEP * (tile + 1) + 6 - shift_here)

            @pl.when(is_this)
            def _(low=low, high=high):
                for l in range(LEVELS):
                    rows = (high - low) * FIELDS
                    source = o_ref.at[l, pl.ds((8 + low) * FIELDS, rows), :]
                    act(pltpu.make_async_copy(source, out_hbm.at[l, pl.ds(low * FIELDS, rows), :], out_sem))

    for g in range(2):
        for side in range(2):
            tile = TILES[g][side]
            for k in range(3):
                for f in range(FIELDS):
                    at, row = g * 3 + k, 2 * f + side
                    west = s_ref[at, pl.ds(EDGE * 8 + row, WIDE, stride=8), :]
                    inner = done_ref[at, pl.ds(WIDE * 8 + row, LON - 2 * WIDE, stride=8), :]
                    east = s_ref[6 + at, pl.ds((EDGE - WIDE) * 8 + row, WIDE, stride=8), :]
                    w_ref[f] = jnp.concatenate([west, inner, east], axis=0).T
                    for l in range(LEVELS):
                        start = (8 + TILE_STEP * tile + 6 + k - shift) * FIELDS + f
                        o_ref[l, pl.ds(start, 38, stride=3 * FIELDS), :] = w_ref[f, pl.ds(CHUNKS * l + 2, 38), :]
            write_rows(tile, lambda copy: copy.start())
    for tile in range(4):
        write_rows(tile, lambda copy: copy.wait())


def run_outer(table, cz, cm, from_west, from_east, done, state, step):
    args = [pltpu.with_memory_space_constraint(x, pltpu.VMEM) for x in (table, cz, cm, from_west, from_east, done, state, step)]
    return pl.pallas_call(
        outer_kernel,
        out_shape=jax.ShapeDtypeStruct((LEVELS, ROWS * FIELDS, LON), jnp.float32),
        in_specs=[pl.BlockSpec(memory_space=pltpu.VMEM)] * len(args),
        out_specs=pl.BlockSpec(memory_space=pl.ANY),
        scratch_shapes=[
            pltpu.VMEM((12, 2 * EDGE * 8, 128), jnp.float32),
            pltpu.VMEM((8, 2 * EDGE * 8, 128), jnp.float32),
            pltpu.VMEM((2 * C_SIZE, 2 * EDGE * 8, 128), jnp.float32),
            pltpu.VMEM((FIELDS, 128, 128), jnp.float32),
            pltpu.VMEM((LEVELS, 472 * FIELDS, LON), jnp.float32),
            pltpu.SemaphoreType.DMA,
        ],
        compiler_params=pltpu.CompilerParams(vmem_limit_bytes=VMEM_BYTES),
        name="outer_columns",
    )(*args)


def shards(table, tracers, zonal, merid):
    tracers = tracers.transpose(1, 2, 0, 3).reshape(LEVELS, ROWS * FIELDS, LON)
    su, sv, zonal, merid = row_payload(tracers, zonal, merid)
    middle = pack_middle(tracers, zonal, merid, su)
    within, beyond = [], []
    for lon in range(LOOP):
        for band in range(BANDS):
            within.append((lon * BANDS + band, lon * BANDS + (band ^ 1)))
            if band in (0, BANDS - 1):
                target = (lon + LOOP // 2) % LOOP * BANDS + band
            else:
                target = lon * BANDS + (3 - band)
            beyond.append((lon * BANDS + band, target))
    ru = lax.ppermute(su, ("lon", "lat"), within)
    rv = lax.ppermute(sv, ("lon", "lat"), beyond)
    cells, cz, cm, to_west, to_east = pack_rims(middle, ru, rv)
    from_east = lax.ppermute(to_west, "lon", [(i, (i - 1) % LOOP) for i in range(LOOP)])
    from_west = lax.ppermute(to_east, "lon", [(i, (i + 1) % LOOP) for i in range(LOOP)])
    done, state, step = run_inner(table, cells, cz, cm)
    advected = run_outer(table, cz, cm, from_west, from_east, done, state, step)
    return advected.reshape(LEVELS, ROWS, FIELDS, LON).transpose(2, 0, 1, 3)


def solution(mesh):
    table = lane_tables()
    spec, out_spec = P("lev", "lat", "lon"), P(None, "lev", "lat", "lon")

    def run(tracers, zonal_courant, merid_courant):
        inner = functools.partial(shards, jnp.asarray(table))
        return jax.shard_map(inner, mesh=mesh, in_specs=(out_spec, spec, spec), out_specs=out_spec, check_vma=False)(
            tracers, zonal_courant, merid_courant
        )

    return run
```

```python
import functools

import jax
import jax.numpy as jnp
import numpy as np
from jax import lax
from jax.experimental import pallas as pl
from jax.experimental.pallas import tpu as pltpu
from jax.sharding import PartitionSpec as P

FIELDS, LEVELS = 4, 3
NSUB, NSTEPS, PCAP = 4, 3, 224
BANDS, LOOP = 4, 16
ROWS, LON = 450, 128
GLOBE = ROWS * BANDS
CHUNKS, TILE_STEP = 42, 114
TILES = ((0, 1), (3, 2))
SHIFT_NORTH, SHIFT = 12, 6
E_OWN, E_ROWS = 24, 512
WIDE, NARROW, WIDE_Z, WIDE_M, NARROW_Z, NARROW_M = 24, 6, 23, 16, 5, 4
PAYLOAD = 3 * WIDE + 3 * NARROW + WIDE_Z + WIDE_M + NARROW_Z + NARROW_M
RIM = 24
KEEP, EDGE = 10, 32
INNER_COLS = LON + 16
VMEM_BYTES = 24 * 2**20


def lane_tables():
    band = np.arange(BANDS).reshape(-1, 1, 1, 1, 1)
    tile = np.array(TILES).reshape(1, 2, 1, 2, 1)[:, :, :, np.arange(8) % 2]
    k = np.arange(3).reshape(1, 1, 3, 1, 1)
    chunk = (np.arange(128) % CHUNKS).reshape(1, 1, 1, 1, -1)
    shift = np.where(band == BANDS - 1, SHIFT_NORTH, SHIFT)
    row = band * ROWS + TILE_STEP * tile + 3 * chunk + k - shift
    face = np.where(row % GLOBE == 0, 0.0, np.abs(np.sin(np.pi * row / GLOBE)))
    cell = np.abs(np.sin(np.pi * (row + 0.5) / GLOBE))
    group = np.arange(2).reshape(1, 2, 1, 1, 1)
    polar = (band == 0) & (group == 0) | (band == BANDS - 1) & (group == 1)
    cap = polar & ((row < PCAP) | (row >= GLOBE - PCAP))
    kinds = [face / 6.0, 1.0 / cell, np.where(cap, 1.0 / NSUB, 1.0) / 6.0, cap]
    return np.stack([np.broadcast_to(x, row.shape) for x in kinds], axis=1).astype(np.float32)


def row_payload_kernel(t_hbm, z_hbm, m_hbm, u_ref, v_ref, z_ref, m_ref, rim_ref, sems):
    even = lax.axis_index("lat") % 2 == 0
    last = ROWS * FIELDS - RIM
    copies = [
        pltpu.make_async_copy(z_hbm, z_ref, sems.at[0]),
        pltpu.make_async_copy(m_hbm, m_ref, sems.at[1]),
        pltpu.make_async_copy(t_hbm.at[:, pl.ds(0, RIM), :], rim_ref.at[0], sems.at[2]),
        pltpu.make_async_copy(t_hbm.at[:, pl.ds(last, RIM), :], rim_ref.at[1], sems.at[3]),
    ]
    for copy in copies:
        copy.start()
    for copy in copies:
        copy.wait()

    def put(l, first, south, north):
        u_ref[l, first : first + south.shape[0]] = jnp.where(even, north, south)
        v_ref[l, first : first + south.shape[0]] = jnp.where(even, south, north)

    for l in range(LEVELS):
        put(l, 0, rim_ref[0, l], rim_ref[1, l])
        put(l, RIM, z_ref[l, :8], z_ref[l, ROWS - 8 :])
        put(l, RIM + 8, m_ref[l, :8], m_ref[l, ROWS - 8 :])


def row_payload(tracers, zonal, merid):
    shapes = [(LEVELS, RIM + 16, LON)] * 2 + [(LEVELS, ROWS, LON)] * 2
    return pl.pallas_call(
        row_payload_kernel,
        out_shape=[pltpu.VMEM(shape, jnp.float32) for shape in shapes],
        in_specs=[pl.BlockSpec(memory_space=pltpu.HBM)] * 3,
        out_specs=[pl.BlockSpec(memory_space=pltpu.VMEM)] * len(shapes),
        scratch_shapes=[pltpu.VMEM((2, LEVELS, RIM, LON), jnp.float32), pltpu.SemaphoreType.DMA((4,))],
        compiler_params=pltpu.CompilerParams(vmem_limit_bytes=8 * 2**20),
        name="row_payload",
    )(*[pltpu.with_memory_space_constraint(x, pltpu.HBM) for x in (tracers, zonal, merid)])


def pack_side(side, band, t_ref, e_ref, d_ref, cz_ref, cm_ref):
    base = jnp.where(band == BANDS - 1, E_OWN - SHIFT_NORTH, E_OWN - SHIFT)
    sub = lax.broadcasted_iota(jnp.int32, (8, 128), 0)

    def packed(ref, image, start, per_row):
        x, y, z = (ref[image + l, pl.ds(start - 6 * per_row * l, 48, stride=3 * per_row), :] for l in range(3))
        rows = [x[:40], jnp.where(sub < 2, x[40:], y[:8]), y[8:40], jnp.where(sub < 4, y[40:], z[:8]), z[8:]]
        return jnp.concatenate(rows, axis=0).T

    for g in range(2):
        for k in range(3):
            start = base + TILE_STEP * TILES[g][side] + k
            for f in range(FIELDS):
                d_ref[g * 3 + k, pl.ds(2 * f + side, LON, stride=8), :] = packed(t_ref, 0, start * FIELDS + f, FIELDS)
            cz_ref[g, pl.ds(2 * k + side, LON, stride=8), :] = packed(e_ref, 0, start, 1)
            cm_ref[g, pl.ds(2 * k + side, LON, stride=8), :] = packed(e_ref, LEVELS, start, 1)


def pack_middle_kernel(t_hbm, z_ref, m_ref, after_ref, t_ref, e_ref, d_ref, cz_ref, cm_ref, sems):
    copies = []
    for l in range(LEVELS):
        own = t_ref.at[l, pl.ds(E_OWN * FIELDS, ROWS * FIELDS), :]
        copies.append(pltpu.make_async_copy(t_hbm.at[l], own, sems.at[l]))
        copies[l].start()
    north_end = E_OWN + ROWS
    for l in range(LEVELS):
        t_ref[l, : 4 * E_OWN] = jnp.zeros((4 * E_OWN, LON), jnp.float32)
        t_ref[l, 4 * north_end :] = jnp.zeros((4 * (E_ROWS - north_end), LON), jnp.float32)
        for i, ref in ((l, z_ref), (LEVELS + l, m_ref)):
            e_ref[i, :E_OWN] = jnp.zeros((E_OWN, LON), jnp.float32)
            e_ref[i, E_OWN:north_end] = ref[l]
            e_ref[i, north_end:] = jnp.zeros((E_ROWS - north_end, LON), jnp.float32)
    for copy in copies:
        copy.wait()
    pack_side(1, lax.axis_index("lat"), t_ref, e_ref, d_ref, cz_ref, cm_ref)


ROW_SHAPES = [(LEVELS, E_ROWS * FIELDS, LON), (2 * LEVELS, E_ROWS, LON)]
CELL_SHAPES = [(6, INNER_COLS * 8, 128), (2, (LON + 1) * 8, 128), (2, (LON + 1) * 8, 128)]


def pack_middle(tracers, zonal, merid, after):
    shapes = ROW_SHAPES + CELL_SHAPES
    args = [pltpu.with_memory_space_constraint(tracers, pltpu.HBM)]
    args += [pltpu.with_memory_space_constraint(x, pltpu.VMEM) for x in (zonal, merid, after)]
    return pl.pallas_call(
        pack_middle_kernel,
        out_shape=[pltpu.VMEM(shape, jnp.float32) for shape in shapes],
        in_specs=[pl.BlockSpec(memory_space=pltpu.HBM)] + [pl.BlockSpec(memory_space=pltpu.VMEM)] * 3,
        out_specs=[pl.BlockSpec(memory_space=pltpu.VMEM)] * len(shapes),
        scratch_shapes=[pltpu.SemaphoreType.DMA((LEVELS,))],
        compiler_params=pltpu.CompilerParams(vmem_limit_bytes=8 * 2**20),
        name="pack_middle",
    )(*args)


def pack_rims_kernel(t_in, e_in, d_in, cz_in, cm_in, ru, rv, t_ref, e_ref, d_ref, cz_ref, cm_ref, sw_ref, se_ref):
    band = lax.axis_index("lat")
    even = band % 2 == 0
    north_end = E_OWN + ROWS
    for l in range(LEVELS):
        u, v = ru[l, :RIM], rv[l, :RIM]
        t_ref[l, 4 * E_OWN - RIM : 4 * E_OWN] = jnp.where(even, v, u)
        t_ref[l, 4 * north_end : 4 * north_end + RIM] = jnp.where(even, u, v)
        for i, at in ((l, RIM), (LEVELS + l, RIM + 8)):
            u, v = ru[l, at : at + 8], rv[l, at : at + 8]
            e_ref[i, E_OWN - 8 : E_OWN] = jnp.where(even, v, u)
            e_ref[i, north_end : north_end + 8] = jnp.where(even, u, v)

    def mirrored(start, t_start):
        for l in range(LEVELS):
            for h in range(RIM // 4):
                t_ref[l, t_start + 4 * h : t_start + 4 * (h + 1)] = rv[l, RIM - 4 * (h + 1) : RIM - 4 * h]
            for h in range(8):
                e_ref[l, start + h : start + h + 1] = rv[l, RIM + 7 - h : RIM + 8 - h]
                if h > 0:
                    e_ref[LEVELS + l, start + h : start + h + 1] = -rv[l, RIM + 16 - h : RIM + 17 - h]
                else:
                    e_ref[LEVELS + l, start : start + 1] = jnp.zeros((1, LON), jnp.float32)

    @pl.when(band == 0)
    def _():
        mirrored(E_OWN - 8, 4 * E_OWN - RIM)

    @pl.when(band == BANDS - 1)
    def _():
        mirrored(north_end, 4 * north_end)

    pack_side(0, band, t_ref, e_ref, d_ref, cz_ref, cm_ref)
    wide = jnp.where(band == BANDS - 1, 1, 0)
    thin = 1 - wide

    def payload(out, east):
        at = 0

        def put(ref, index, width):
            nonlocal at
            first = LON - width if east else 0
            out[pl.ds(at * 8, width * 8), :] = ref[index, pl.ds(first * 8, width * 8), :]
            at += width

        for k in range(3):
            put(d_ref, wide * 3 + k, WIDE)
        for k in range(3):
            put(d_ref, thin * 3 + k, NARROW)
        put(cz_ref, wide, WIDE_Z)
        put(cm_ref, wide, WIDE_M)
        put(cz_ref, thin, NARROW_Z)
        put(cm_ref, thin, NARROW_M)

    payload(sw_ref, False)
    payload(se_ref, True)


def pack_rims(middle, ru, rv):
    shapes = ROW_SHAPES + CELL_SHAPES + [(PAYLOAD * 8, 128)] * 2
    return vmem_call(pack_rims_kernel, shapes, [], "pack_rims", {i: i for i in range(5)})(*middle, ru, rv)[2:]


def vmem_call(kernel, shapes, scratch, name, aliases=None):
    vmem = pl.BlockSpec(memory_space=pltpu.VMEM)

    def call(*args):
        return pl.pallas_call(
            kernel,
            out_shape=[pltpu.VMEM(shape, jnp.float32) for shape in shapes],
            in_specs=[vmem] * len(args),
            out_specs=[vmem] * len(shapes),
            scratch_shapes=scratch,
            input_output_aliases=aliases or {},
            compiler_params=pltpu.CompilerParams(vmem_limit_bytes=VMEM_BYTES),
            name=name,
        )(*[pltpu.with_memory_space_constraint(x, pltpu.VMEM) for x in args])

    return call


def upwind(c, a, b, d, e, b3, d3):
    s = b + d
    return c * ((s + s) + jnp.where(c > 0, b3 - a, d3 - e))


def block(ref, index, first, count):
    return ref[index, pl.ds(pl.multiple_of(first * 8, 8), count * 8), :].reshape(count, 8, 128)


def put_block(ref, index, first, value):
    count = value.shape[0]
    ref[index, pl.ds(pl.multiple_of(first * 8, 8), count * 8), :] = value.reshape(count * 8, 128)


def columns(ref, index, first, count):
    return ref.at[index, pl.ds(pl.multiple_of(first * 8, 8), count * 8), :]


def side_one():
    return lax.broadcasted_iota(jnp.int32, (8, 128), 0) % 2 == 1


def roll(x, steps):
    return pltpu.roll(x.reshape(-1, 128), steps, 1).reshape(x.shape)


def spread(source, source_at, out, out_at, scale, first, chunks, masked_at=None, masks=None):
    odd = side_one()

    def body(j, carry):
        for u in range(8):
            i = first + j * 8 + u
            for k in range(3):
                low = source[source_at, pl.ds(i * 8 + 2 * k, 1), :]
                high = source[source_at, pl.ds(i * 8 + 2 * k + 1, 1), :]
                both = jnp.where(odd, jnp.broadcast_to(high, (8, 128)), jnp.broadcast_to(low, (8, 128))) * scale[k]
                put_block(out, out_at + k, i, both[None])
                if masks is not None:
                    put_block(out, masked_at + k, i, (both * masks[k])[None])
        return carry

    lax.fori_loop(0, chunks, body, 0)


def sweeps(s_ref, c_ref, r_ref, count, unroll, zonal=(), meridional=(), inverse=None, band=None, ahead=True):
    def begin(at, c_at, first):
        p = block(s_ref, at, first - 2, 4)
        flux = upwind(block(c_ref, c_at, first, 1)[0], p[0], p[1], p[2], p[3], 3.0 * p[1], 3.0 * p[2])
        return flux[None], p[1:2]

    if band is not None:
        north = band == BANDS - 1
        turn = jnp.where(north, 38, 90)
        chunk = jnp.where(north, CHUNKS - 1, 0)
        k_first = jnp.where(north, 1, 0)
        lane = lax.broadcasted_iota(jnp.int32, (8, 128), 1)
        hit = side_one() & ((lane == chunk) | (lane == chunk + CHUNKS) | (lane == chunk + 2 * CHUNKS))
        hits = [hit & (k_first <= k) & (k <= k_first + 1) for k in range(3)]

    def prepared(n, at, i):
        p = [block(s_ref, at + k, i, unroll) for k in range(3)]
        moves = [roll(p[1], 1), roll(p[2], 1), roll(p[0], 127)]
        results = [(r_ref, n * 6 + slot, i, value) for slot, value in enumerate(moves)]
        if band is not None and ahead:
            for k in (k_first, k_first + 1):
                results.append((r_ref, n * 6 + 3 + k, i, roll(block(s_ref, at + k, i, unroll), turn)))
        elif band is not None:
            results.extend((r_ref, n * 6 + 3 + k, i, roll(p[k], turn)) for k in range(3))
        return results

    def store(results):
        for ref, where, i, value in results:
            put_block(ref, where, i, value)

    if ahead:
        for n, (at, c_at, first) in enumerate(meridional):
            store(prepared(n, at, first))

    def body(j, carry):
        results, after, begun, moved = [], [], [], []
        for n, (at, c_at, first) in enumerate(meridional):
            i = first + j * unroll
            p = [block(s_ref, at + k, i, unroll) for k in range(3)]
            if ahead:
                moves = [block(r_ref, n * 6 + slot, i, unroll) for slot in range(3 if band is None else 6)]
                store(prepared(n, at, i + unroll))
            else:
                moves = [value for _, _, _, value in prepared(n, at, i)]
            c0, below, twice_below = block(c_ref, c_at, i, unroll), moves[0], moves[1]
            t0 = 3.0 * p[0]
            f0 = upwind(c0, below, twice_below, p[0], p[1], 3.0 * twice_below, t0)
            begun.append((i, p, t0, f0, roll(f0, 127), twice_below, moves[2]))
            moved.extend(moves[3:])
        for (at, c_at, _), (i, (p0, p1, p2), t0, f0, f0_above, p2_below, p0_above) in zip(meridional, begun, strict=True):
            c1, c2 = (block(c_ref, c_at + k, i, unroll) for k in (1, 2))
            t1, t2 = 3.0 * p1, 3.0 * p2
            f1 = upwind(c1, p2_below, p0, p1, p2, t0, t1)
            f2 = upwind(c2, p0, p1, p2, p0_above, t1, t2)
            results.append((s_ref, at, i, p0 - (f1 - f0) * inverse[0]))
            results.append((s_ref, at + 1, i, p1 - (f2 - f1) * inverse[1]))
            results.append((s_ref, at + 2, i, p2 - (f0_above - f2) * inverse[2]))
        for n, (at, c_at, first) in enumerate(zonal):
            i = first + j * unroll
            for k in range(3):
                flux_before, before = carry[n * 3 + k]
                p = jnp.concatenate([before, block(s_ref, at + k, i, unroll + 2)], axis=0)
                c = block(c_ref, c_at + k, i + 1, unroll)
                p3 = 3.0 * p[1 : unroll + 2]
                flux = upwind(c, p[:unroll], p[1 : unroll + 1], p[2 : unroll + 2], p[3:], p3[:-1], p3[1:])
                west = jnp.concatenate([flux_before, flux[:-1]], axis=0)
                value = p[1 : unroll + 1] - (flux - west)
                if band is not None:
                    value = jnp.where(hits[k], moved[n * 3 + k], value)
                results.append((s_ref, at + k, i, value))
                after.append((flux[-1:], p[unroll : unroll + 1]))
        store(results)
        return tuple(after)

    carry = tuple(begin(at + k, c_at + k, first) for at, c_at, first in zonal for k in range(3))
    if count == 1:
        body(0, carry)
    else:
        lax.fori_loop(0, count, body, carry)


ZONAL_WIDE, ZONAL_MASKED, ZONAL_THIN, MERID_WIDE, MERID_THIN, C_SIZE = 0, 3, 6, 9, 12, 15


def spread_all(tab, band, wide, thin, out, base, zonal, merid, spans):
    for g, span, zonal_at, merid_at in ((wide, spans[0], ZONAL_WIDE, MERID_WIDE), (thin, spans[1], ZONAL_THIN, MERID_THIN)):
        scale, weight, cap = ([tab[band, kind, g, k] for k in range(3)] for kind in (2, 0, 3))
        masked = (base + ZONAL_MASKED, cap) if g is wide else ()
        spread(zonal[0], zonal[1] + g, out, base + zonal_at, scale, *span, *masked)
        spread(merid[0], merid[1] + g, out, base + merid_at, weight, *spans[2])


def keep(state_ref, s_ref, cycle, group):
    edge = 8 * cycle
    for k in range(3):
        i = group * 3 + k
        put_block(state_ref, cycle * 6 + i, 0, block(s_ref, i, edge, KEEP))
        put_block(state_ref, cycle * 6 + i, KEEP, block(s_ref, i, LON - edge - KEEP, KEEP))


def inner_kernel(tab, d_ref, cz_ref, cm_ref, s_ref, state_ref, step_ref, c_ref, r_ref):
    band = lax.axis_index("lat")
    is_cap = (band == 0) | (band == BANDS - 1)
    wide = jnp.where(band == BANDS - 1, 1, 0)
    thin = 1 - wide
    at_wide, at_thin = wide * 3, thin * 3
    inverse_wide, inverse_thin = ([tab[band, 1, g, k] for k in range(3)] for g in (wide, thin))
    spread_all(tab, band, wide, thin, c_ref, 0, (cz_ref, 0), (cm_ref, 0), ((0, LON // 8), (8, LON // 8 - 1), (8, LON // 8 - 2)))
    keep(state_ref, s_ref, 0, wide)
    keep(state_ref, s_ref, 0, thin)
    sweeps(s_ref, c_ref, r_ref, 4, LON // 4 - 1, [(at_wide, ZONAL_WIDE, 2)])

    for cycle in range(NSTEPS):
        edge = 8 * (cycle + 1)
        kept = LON - 2 * edge

        @pl.when(is_cap)
        def _(cycle=cycle):
            for sub in range(1, NSUB + 1):
                low = 2 * (NSUB * cycle + sub)
                if sub > 1:
                    width = LON - 2 * low
                    unroll = max(n for n in range(8, 31) if width % n == 0)
                    sweeps(s_ref, c_ref, r_ref, width // unroll, unroll, [(at_wide, ZONAL_MASKED, low)])
                if sub < NSUB:
                    for k in range(3):
                        at = (cycle * 3 + sub - 1) * 3 + k
                        put_block(step_ref, at, 0, block(s_ref, at_wide + k, low, 4))
                        put_block(step_ref, at, 4, block(s_ref, at_wide + k, LON - low - 4, 4))

        beside = band if cycle == 0 else None
        sweeps(s_ref, c_ref, r_ref, kept // 16, 16, [(at_thin, ZONAL_THIN, edge)], [(at_wide, MERID_WIDE, edge)], inverse_wide, beside)
        if cycle < NSTEPS - 1:
            keep(state_ref, s_ref, cycle + 1, wide)
            then = [(at_wide, ZONAL_WIDE, edge + 2)]
        else:
            then = []
        sweeps(s_ref, c_ref, r_ref, kept // 16, 16, then, [(at_thin, MERID_THIN, edge)], inverse_thin)
        if cycle < NSTEPS - 1:
            keep(state_ref, s_ref, cycle + 1, thin)


def run_inner(table, cells, cz, cm):
    shapes = [(6, INNER_COLS * 8, 128), (18, 2 * KEEP * 8, 128), (27, 64, 128)]
    scratch = [pltpu.VMEM((n, INNER_COLS * 8, 128), jnp.float32) for n in (C_SIZE, 6)]
    return vmem_call(inner_kernel, shapes, scratch, "inner_columns", {1: 0})(table, cells, cz, cm)


def outer_kernel(tab, cz_ref, cm_ref, rw_ref, re_ref, done_ref, state_ref, step_ref, out_hbm, s_ref, cu_ref, c_ref, w_ref, o_ref, out_sem):
    band = lax.axis_index("lat")
    is_cap = (band == 0) | (band == BANDS - 1)
    wide = jnp.where(band == BANDS - 1, 1, 0)
    thin = 1 - wide
    for g in range(2):
        for kind, own in ((0, cz_ref), (1, cm_ref)):
            put_block(cu_ref, kind * 2 + g, EDGE, block(own, g, 0, EDGE))
            put_block(cu_ref, 4 + kind * 2 + g, 0, block(own, g, LON - EDGE, EDGE))
    for side, recv in ((0, rw_ref), (1, re_ref)):
        at = 0
        plan = [(s_ref, side * 6 + wide * 3 + k, WIDE) for k in range(3)]
        plan += [(s_ref, side * 6 + thin * 3 + k, NARROW) for k in range(3)]
        plan += [(cu_ref, side * 4 + wide, WIDE_Z), (cu_ref, side * 4 + 2 + wide, WIDE_M)]
        plan += [(cu_ref, side * 4 + thin, NARROW_Z), (cu_ref, side * 4 + 2 + thin, NARROW_M)]
        for ref, index, width in plan:
            first = EDGE if side else EDGE - width
            put_block(ref, index, first, recv[at * 8 : (at + width) * 8, :].reshape(width, 8, 128))
            at += width

    def take(cycle, group):
        edge = 8 * cycle
        for k in range(3):
            i = group * 3 + k
            put_block(s_ref, i, EDGE + edge, block(state_ref, cycle * 6 + i, 0, KEEP))
            put_block(s_ref, 6 + i, EDGE - edge - KEEP, block(state_ref, cycle * 6 + i, KEEP, KEEP))

    def places(at, c_at, first):
        return [(side * 6 + at, side * C_SIZE + c_at, first[side]) for side in range(2)]

    def sweep(zonal, meridional=(), inverse=None, beside=None):
        sweeps(s_ref, c_ref, None, 2, 12, zonal, meridional, inverse, beside, ahead=False)

    def first_zonal(cycle):
        low = jnp.where(is_cap, 8 * cycle + 2, 8 * cycle + 8)
        return places(at_wide, ZONAL_WIDE, (EDGE - WIDE + low, EDGE - low))

    at_wide, at_thin = wide * 3, thin * 3
    inverse_wide, inverse_thin = ([tab[band, 1, g, k] for k in range(3)] for g in (wide, thin))
    for side in range(2):
        near = EDGE - WIDE + (0 if side else 8)
        spans = ((EDGE - WIDE, 6 if side else 7), (near, 6), (near, 5))
        spread_all(tab, band, wide, thin, c_ref, side * C_SIZE, (cu_ref, side * 4), (cu_ref, side * 4 + 2), spans)
    take(0, wide)
    take(0, thin)
    sweep(first_zonal(0))

    for cycle in range(NSTEPS):
        edge = 8 * (cycle + 1)
        first = (EDGE - WIDE + edge, EDGE - edge)

        @pl.when(is_cap)
        def _(cycle=cycle):
            for sub in range(1, NSUB + 1):
                low = 2 * (NSUB * cycle + sub)
                if sub > 1:
                    sweep(places(at_wide, ZONAL_MASKED, (EDGE - WIDE + low, EDGE - low)))
                if sub < NSUB:
                    for k in range(3):
                        at = (cycle * 3 + sub - 1) * 3 + k
                        put_block(s_ref, at_wide + k, EDGE + low, block(step_ref, at, 0, 4))
                        put_block(s_ref, 6 + at_wide + k, EDGE - low - 4, block(step_ref, at, 4, 4))

        beside = band if cycle == 0 else None
        sweep(places(at_thin, ZONAL_THIN, first), places(at_wide, MERID_WIDE, first), inverse_wide, beside)
        if cycle < NSTEPS - 1:
            take(cycle + 1, wide)
            then = first_zonal(cycle + 1)
        else:
            then = []
        sweep(then, places(at_thin, MERID_THIN, first), inverse_thin)
        if cycle < NSTEPS - 1:
            take(cycle + 1, thin)

    north = band == BANDS - 1
    shift = jnp.where(north, SHIFT_NORTH, SHIFT)

    def write_rows(tile, act):
        for is_this, shift_here in ((north, SHIFT_NORTH), (jnp.logical_not(north), SHIFT)):
            low = max(0, TILE_STEP * tile + 6 - shift_here)
            high = min(ROWS, TILE_STEP * (tile + 1) + 6 - shift_here)

            @pl.when(is_this)
            def _(low=low, high=high):
                for l in range(LEVELS):
                    rows = (high - low) * FIELDS
                    source = o_ref.at[l, pl.ds((8 + low) * FIELDS, rows), :]
                    act(pltpu.make_async_copy(source, out_hbm.at[l, pl.ds(low * FIELDS, rows), :], out_sem))

    for g in range(2):
        for side in range(2):
            tile = TILES[g][side]
            for k in range(3):
                for f in range(FIELDS):
                    at, row = g * 3 + k, 2 * f + side
                    west = s_ref[at, pl.ds(EDGE * 8 + row, WIDE, stride=8), :]
                    inner = done_ref[at, pl.ds(WIDE * 8 + row, LON - 2 * WIDE, stride=8), :]
                    east = s_ref[6 + at, pl.ds((EDGE - WIDE) * 8 + row, WIDE, stride=8), :]
                    w_ref[f] = jnp.concatenate([west, inner, east], axis=0).T
                    for l in range(LEVELS):
                        start = (8 + TILE_STEP * tile + 6 + k - shift) * FIELDS + f
                        o_ref[l, pl.ds(start, 38, stride=3 * FIELDS), :] = w_ref[f, pl.ds(CHUNKS * l + 2, 38), :]
            write_rows(tile, lambda copy: copy.start())
    for tile in range(4):
        write_rows(tile, lambda copy: copy.wait())


def run_outer(table, cz, cm, from_west, from_east, done, state, step):
    args = [pltpu.with_memory_space_constraint(x, pltpu.VMEM) for x in (table, cz, cm, from_west, from_east, done, state, step)]
    return pl.pallas_call(
        outer_kernel,
        out_shape=jax.ShapeDtypeStruct((LEVELS, ROWS * FIELDS, LON), jnp.float32),
        in_specs=[pl.BlockSpec(memory_space=pltpu.VMEM)] * len(args),
        out_specs=pl.BlockSpec(memory_space=pl.ANY),
        scratch_shapes=[
            pltpu.VMEM((12, 2 * EDGE * 8, 128), jnp.float32),
            pltpu.VMEM((8, 2 * EDGE * 8, 128), jnp.float32),
            pltpu.VMEM((2 * C_SIZE, 2 * EDGE * 8, 128), jnp.float32),
            pltpu.VMEM((FIELDS, 128, 128), jnp.float32),
            pltpu.VMEM((LEVELS, 472 * FIELDS, LON), jnp.float32),
            pltpu.SemaphoreType.DMA,
        ],
        compiler_params=pltpu.CompilerParams(vmem_limit_bytes=VMEM_BYTES),
        name="outer_columns",
    )(*args)


def shards(table, tracers, zonal, merid):
    tracers = tracers.transpose(1, 2, 0, 3).reshape(LEVELS, ROWS * FIELDS, LON)
    su, sv, zonal, merid = row_payload(tracers, zonal, merid)
    middle = pack_middle(tracers, zonal, merid, su)
    within, beyond = [], []
    for lon in range(LOOP):
        for band in range(BANDS):
            within.append((lon * BANDS + band, lon * BANDS + (band ^ 1)))
            if band in (0, BANDS - 1):
                target = (lon + LOOP // 2) % LOOP * BANDS + band
            else:
                target = lon * BANDS + (3 - band)
            beyond.append((lon * BANDS + band, target))
    ru = lax.ppermute(su, ("lon", "lat"), within)
    rv = lax.ppermute(sv, ("lon", "lat"), beyond)
    cells, cz, cm, to_west, to_east = pack_rims(middle, ru, rv)
    from_east = lax.ppermute(to_west, "lon", [(i, (i - 1) % LOOP) for i in range(LOOP)])
    from_west = lax.ppermute(to_east, "lon", [(i, (i + 1) % LOOP) for i in range(LOOP)])
    done, state, step = run_inner(table, cells, cz, cm)
    advected = run_outer(table, cz, cm, from_west, from_east, done, state, step)
    return advected.reshape(LEVELS, ROWS, FIELDS, LON).transpose(2, 0, 1, 3)


def solution(mesh):
    table = lane_tables()
    spec, out_spec = P("lev", "lat", "lon"), P(None, "lev", "lat", "lon")

    def run(tracers, zonal_courant, merid_courant):
        inner = functools.partial(shards, jnp.asarray(table))
        return jax.shard_map(inner, mesh=mesh, in_specs=(out_spec, spec, spec), out_specs=out_spec, check_vma=False)(
            tracers, zonal_courant, merid_courant
        )

    return run
```

```python
import functools

import jax
import jax.numpy as jnp
import numpy as np
from jax import lax
from jax.experimental import pallas as pl
from jax.experimental.pallas import tpu as pltpu
from jax.sharding import PartitionSpec as P

FIELDS, LEVELS = 4, 3
NSUB, NSTEPS, PCAP = 4, 3, 224
BANDS, LOOP = 4, 16
ROWS, LON = 450, 128
GLOBE = ROWS * BANDS
CHUNKS, TILE_STEP = 42, 114
TILES = ((0, 1), (3, 2))
SHIFT_NORTH, SHIFT = 12, 6
E_OWN, E_ROWS = 24, 512
WIDE, NARROW, WIDE_Z, WIDE_M, NARROW_Z, NARROW_M = 24, 6, 23, 16, 5, 4
PAYLOAD = 3 * WIDE + 3 * NARROW + WIDE_Z + WIDE_M + NARROW_Z + NARROW_M
RIM = 24
KEEP, EDGE = 10, 32
INNER_COLS = LON + 16
VMEM_BYTES = 24 * 2**20


def lane_tables():
    band = np.arange(BANDS).reshape(-1, 1, 1, 1, 1)
    tile = np.array(TILES).reshape(1, 2, 1, 2, 1)[:, :, :, np.arange(8) % 2]
    k = np.arange(3).reshape(1, 1, 3, 1, 1)
    chunk = (np.arange(128) % CHUNKS).reshape(1, 1, 1, 1, -1)
    shift = np.where(band == BANDS - 1, SHIFT_NORTH, SHIFT)
    row = band * ROWS + TILE_STEP * tile + 3 * chunk + k - shift
    face = np.where(row % GLOBE == 0, 0.0, np.abs(np.sin(np.pi * row / GLOBE)))
    cell = np.abs(np.sin(np.pi * (row + 0.5) / GLOBE))
    group = np.arange(2).reshape(1, 2, 1, 1, 1)
    polar = (band == 0) & (group == 0) | (band == BANDS - 1) & (group == 1)
    cap = polar & ((row < PCAP) | (row >= GLOBE - PCAP))
    kinds = [face / 6.0, 1.0 / cell, np.where(cap, 1.0 / NSUB, 1.0) / 6.0, cap]
    return np.stack([np.broadcast_to(x, row.shape) for x in kinds], axis=1).astype(np.float32)


def row_payload_kernel(t_hbm, z_hbm, m_hbm, u_ref, v_ref, z_ref, m_ref, rim_ref, sems):
    even = lax.axis_index("lat") % 2 == 0
    last = ROWS * FIELDS - RIM
    copies = [
        pltpu.make_async_copy(z_hbm, z_ref, sems.at[0]),
        pltpu.make_async_copy(m_hbm, m_ref, sems.at[1]),
        pltpu.make_async_copy(t_hbm.at[:, pl.ds(0, RIM), :], rim_ref.at[0], sems.at[2]),
        pltpu.make_async_copy(t_hbm.at[:, pl.ds(last, RIM), :], rim_ref.at[1], sems.at[3]),
    ]
    for copy in copies:
        copy.start()
    for copy in copies:
        copy.wait()

    def put(l, first, south, north):
        u_ref[l, first : first + south.shape[0]] = jnp.where(even, north, south)
        v_ref[l, first : first + south.shape[0]] = jnp.where(even, south, north)

    for l in range(LEVELS):
        put(l, 0, rim_ref[0, l], rim_ref[1, l])
        put(l, RIM, z_ref[l, :8], z_ref[l, ROWS - 8 :])
        put(l, RIM + 8, m_ref[l, :8], m_ref[l, ROWS - 8 :])


def row_payload(tracers, zonal, merid):
    shapes = [(LEVELS, RIM + 16, LON)] * 2 + [(LEVELS, ROWS, LON)] * 2
    return pl.pallas_call(
        row_payload_kernel,
        out_shape=[pltpu.VMEM(shape, jnp.float32) for shape in shapes],
        in_specs=[pl.BlockSpec(memory_space=pltpu.HBM)] * 3,
        out_specs=[pl.BlockSpec(memory_space=pltpu.VMEM)] * len(shapes),
        scratch_shapes=[pltpu.VMEM((2, LEVELS, RIM, LON), jnp.float32), pltpu.SemaphoreType.DMA((4,))],
        compiler_params=pltpu.CompilerParams(vmem_limit_bytes=8 * 2**20),
        name="row_payload",
    )(*[pltpu.with_memory_space_constraint(x, pltpu.HBM) for x in (tracers, zonal, merid)])


def pack_side(side, band, t_ref, e_ref, d_ref, cz_ref, cm_ref):
    base = jnp.where(band == BANDS - 1, E_OWN - SHIFT_NORTH, E_OWN - SHIFT)
    sub = lax.broadcasted_iota(jnp.int32, (8, 128), 0)

    def packed(ref, image, start, per_row):
        x, y, z = (ref[image + l, pl.ds(start - 6 * per_row * l, 48, stride=3 * per_row), :] for l in range(3))
        rows = [x[:40], jnp.where(sub < 2, x[40:], y[:8]), y[8:40], jnp.where(sub < 4, y[40:], z[:8]), z[8:]]
        return jnp.concatenate(rows, axis=0).T

    for g in range(2):
        for k in range(3):
            start = base + TILE_STEP * TILES[g][side] + k
            for f in range(FIELDS):
                d_ref[g * 3 + k, pl.ds(2 * f + side, LON, stride=8), :] = packed(t_ref, 0, start * FIELDS + f, FIELDS)
            cz_ref[g, pl.ds(2 * k + side, LON, stride=8), :] = packed(e_ref, 0, start, 1)
            cm_ref[g, pl.ds(2 * k + side, LON, stride=8), :] = packed(e_ref, LEVELS, start, 1)


def pack_middle_kernel(t_hbm, z_ref, m_ref, after_ref, t_ref, e_ref, d_ref, cz_ref, cm_ref, sems):
    copies = []
    for l in range(LEVELS):
        own = t_ref.at[l, pl.ds(E_OWN * FIELDS, ROWS * FIELDS), :]
        copies.append(pltpu.make_async_copy(t_hbm.at[l], own, sems.at[l]))
        copies[l].start()
    north_end = E_OWN + ROWS
    for l in range(LEVELS):
        t_ref[l, : 4 * E_OWN] = jnp.zeros((4 * E_OWN, LON), jnp.float32)
        t_ref[l, 4 * north_end :] = jnp.zeros((4 * (E_ROWS - north_end), LON), jnp.float32)
        for i, ref in ((l, z_ref), (LEVELS + l, m_ref)):
            e_ref[i, :E_OWN] = jnp.zeros((E_OWN, LON), jnp.float32)
            e_ref[i, E_OWN:north_end] = ref[l]
            e_ref[i, north_end:] = jnp.zeros((E_ROWS - north_end, LON), jnp.float32)
    for copy in copies:
        copy.wait()
    pack_side(1, lax.axis_index("lat"), t_ref, e_ref, d_ref, cz_ref, cm_ref)


ROW_SHAPES = [(LEVELS, E_ROWS * FIELDS, LON), (2 * LEVELS, E_ROWS, LON)]
CELL_SHAPES = [(6, INNER_COLS * 8, 128), (2, (LON + 1) * 8, 128), (2, (LON + 1) * 8, 128)]


def pack_middle(tracers, zonal, merid, after):
    shapes = ROW_SHAPES + CELL_SHAPES
    args = [pltpu.with_memory_space_constraint(tracers, pltpu.HBM)]
    args += [pltpu.with_memory_space_constraint(x, pltpu.VMEM) for x in (zonal, merid, after)]
    return pl.pallas_call(
        pack_middle_kernel,
        out_shape=[pltpu.VMEM(shape, jnp.float32) for shape in shapes],
        in_specs=[pl.BlockSpec(memory_space=pltpu.HBM)] + [pl.BlockSpec(memory_space=pltpu.VMEM)] * 3,
        out_specs=[pl.BlockSpec(memory_space=pltpu.VMEM)] * len(shapes),
        scratch_shapes=[pltpu.SemaphoreType.DMA((LEVELS,))],
        compiler_params=pltpu.CompilerParams(vmem_limit_bytes=8 * 2**20),
        name="pack_middle",
    )(*args)


def pack_rims_kernel(t_in, e_in, d_in, cz_in, cm_in, ru, rv, t_ref, e_ref, d_ref, cz_ref, cm_ref, sw_ref, se_ref):
    band = lax.axis_index("lat")
    even = band % 2 == 0
    north_end = E_OWN + ROWS
    for l in range(LEVELS):
        u, v = ru[l, :RIM], rv[l, :RIM]
        t_ref[l, 4 * E_OWN - RIM : 4 * E_OWN] = jnp.where(even, v, u)
        t_ref[l, 4 * north_end : 4 * north_end + RIM] = jnp.where(even, u, v)
        for i, at in ((l, RIM), (LEVELS + l, RIM + 8)):
            u, v = ru[l, at : at + 8], rv[l, at : at + 8]
            e_ref[i, E_OWN - 8 : E_OWN] = jnp.where(even, v, u)
            e_ref[i, north_end : north_end + 8] = jnp.where(even, u, v)

    def mirrored(start, t_start):
        for l in range(LEVELS):
            for h in range(RIM // 4):
                t_ref[l, t_start + 4 * h : t_start + 4 * (h + 1)] = rv[l, RIM - 4 * (h + 1) : RIM - 4 * h]
            for h in range(8):
                e_ref[l, start + h : start + h + 1] = rv[l, RIM + 7 - h : RIM + 8 - h]
                if h > 0:
                    e_ref[LEVELS + l, start + h : start + h + 1] = -rv[l, RIM + 16 - h : RIM + 17 - h]
                else:
                    e_ref[LEVELS + l, start : start + 1] = jnp.zeros((1, LON), jnp.float32)

    @pl.when(band == 0)
    def _():
        mirrored(E_OWN - 8, 4 * E_OWN - RIM)

    @pl.when(band == BANDS - 1)
    def _():
        mirrored(north_end, 4 * north_end)

    pack_side(0, band, t_ref, e_ref, d_ref, cz_ref, cm_ref)
    wide = jnp.where(band == BANDS - 1, 1, 0)
    thin = 1 - wide

    def payload(out, east):
        at = 0

        def put(ref, index, width):
            nonlocal at
            first = LON - width if east else 0
            out[pl.ds(at * 8, width * 8), :] = ref[index, pl.ds(first * 8, width * 8), :]
            at += width

        for k in range(3):
            put(d_ref, wide * 3 + k, WIDE)
        for k in range(3):
            put(d_ref, thin * 3 + k, NARROW)
        put(cz_ref, wide, WIDE_Z)
        put(cm_ref, wide, WIDE_M)
        put(cz_ref, thin, NARROW_Z)
        put(cm_ref, thin, NARROW_M)

    payload(sw_ref, False)
    payload(se_ref, True)


def pack_rims(middle, ru, rv):
    shapes = ROW_SHAPES + CELL_SHAPES + [(PAYLOAD * 8, 128)] * 2
    return vmem_call(pack_rims_kernel, shapes, [], "pack_rims", {i: i for i in range(5)})(*middle, ru, rv)[2:]


def vmem_call(kernel, shapes, scratch, name, aliases=None):
    vmem = pl.BlockSpec(memory_space=pltpu.VMEM)

    def call(*args):
        return pl.pallas_call(
            kernel,
            out_shape=[pltpu.VMEM(shape, jnp.float32) for shape in shapes],
            in_specs=[vmem] * len(args),
            out_specs=[vmem] * len(shapes),
            scratch_shapes=scratch,
            input_output_aliases=aliases or {},
            compiler_params=pltpu.CompilerParams(vmem_limit_bytes=VMEM_BYTES),
            name=name,
        )(*[pltpu.with_memory_space_constraint(x, pltpu.VMEM) for x in args])

    return call


def upwind(c, a, b, d, e, b3, d3):
    s = b + d
    return c * ((s + s) + jnp.where(c > 0, b3 - a, d3 - e))


def block(ref, index, first, count):
    return ref[index, pl.ds(pl.multiple_of(first * 8, 8), count * 8), :].reshape(count, 8, 128)


def put_block(ref, index, first, value):
    count = value.shape[0]
    ref[index, pl.ds(pl.multiple_of(first * 8, 8), count * 8), :] = value.reshape(count * 8, 128)


def columns(ref, index, first, count):
    return ref.at[index, pl.ds(pl.multiple_of(first * 8, 8), count * 8), :]


def side_one():
    return lax.broadcasted_iota(jnp.int32, (8, 128), 0) % 2 == 1


def roll(x, steps):
    return pltpu.roll(x.reshape(-1, 128), steps, 1).reshape(x.shape)


def spread(source, source_at, out, out_at, scale, first, chunks, masked_at=None, masks=None):
    odd = side_one()

    def body(j, carry):
        for u in range(8):
            i = first + j * 8 + u
            for k in range(3):
                low = source[source_at, pl.ds(i * 8 + 2 * k, 1), :]
                high = source[source_at, pl.ds(i * 8 + 2 * k + 1, 1), :]
                both = jnp.where(odd, jnp.broadcast_to(high, (8, 128)), jnp.broadcast_to(low, (8, 128))) * scale[k]
                put_block(out, out_at + k, i, both[None])
                if masks is not None:
                    put_block(out, masked_at + k, i, (both * masks[k])[None])
        return carry

    lax.fori_loop(0, chunks, body, 0)


def sweeps(s_ref, c_ref, r_ref, count, unroll, zonal=(), meridional=(), inverse=None, band=None, ahead=True):
    def begin(at, c_at, first):
        p = block(s_ref, at, first - 2, 4)
        flux = upwind(block(c_ref, c_at, first, 1)[0], p[0], p[1], p[2], p[3], 3.0 * p[1], 3.0 * p[2])
        return flux[None], p[1:2]

    if band is not None:
        north = band == BANDS - 1
        turn = jnp.where(north, 38, 90)
        chunk = jnp.where(north, CHUNKS - 1, 0)
        k_first = jnp.where(north, 1, 0)
        lane = lax.broadcasted_iota(jnp.int32, (8, 128), 1)
        hit = side_one() & ((lane == chunk) | (lane == chunk + CHUNKS) | (lane == chunk + 2 * CHUNKS))
        hits = [hit & (k_first <= k) & (k <= k_first + 1) for k in range(3)]

    def prepared(n, at, i):
        p = [block(s_ref, at + k, i, unroll) for k in range(3)]
        moves = [roll(p[1], 1), roll(p[2], 1), roll(p[0], 127)]
        results = [(r_ref, n * 6 + slot, i, value) for slot, value in enumerate(moves)]
        if band is not None and ahead:
            for k in (k_first, k_first + 1):
                results.append((r_ref, n * 6 + 3 + k, i, roll(block(s_ref, at + k, i, unroll), turn)))
        elif band is not None:
            results.extend((r_ref, n * 6 + 3 + k, i, roll(p[k], turn)) for k in range(3))
        return results

    def store(results):
        for ref, where, i, value in results:
            put_block(ref, where, i, value)

    if ahead:
        for n, (at, c_at, first) in enumerate(meridional):
            store(prepared(n, at, first))

    def body(j, carry):
        results, after, begun, moved = [], [], [], []
        for n, (at, c_at, first) in enumerate(meridional):
            i = first + j * unroll
            p = [block(s_ref, at + k, i, unroll) for k in range(3)]
            if ahead:
                moves = [block(r_ref, n * 6 + slot, i, unroll) for slot in range(3 if band is None else 6)]
                store(prepared(n, at, i + unroll))
            else:
                moves = [value for _, _, _, value in prepared(n, at, i)]
            c0, below, twice_below = block(c_ref, c_at, i, unroll), moves[0], moves[1]
            t0 = 3.0 * p[0]
            f0 = upwind(c0, below, twice_below, p[0], p[1], 3.0 * twice_below, t0)
            begun.append((i, p, t0, f0, roll(f0, 127), twice_below, moves[2]))
            moved.extend(moves[3:])
        for (at, c_at, _), (i, (p0, p1, p2), t0, f0, f0_above, p2_below, p0_above) in zip(meridional, begun, strict=True):
            c1, c2 = (block(c_ref, c_at + k, i, unroll) for k in (1, 2))
            t1, t2 = 3.0 * p1, 3.0 * p2
            f1 = upwind(c1, p2_below, p0, p1, p2, t0, t1)
            f2 = upwind(c2, p0, p1, p2, p0_above, t1, t2)
            results.append((s_ref, at, i, p0 - (f1 - f0) * inverse[0]))
            results.append((s_ref, at + 1, i, p1 - (f2 - f1) * inverse[1]))
            results.append((s_ref, at + 2, i, p2 - (f0_above - f2) * inverse[2]))
        for n, (at, c_at, first) in enumerate(zonal):
            i = first + j * unroll
            for k in range(3):
                flux_before, before = carry[n * 3 + k]
                p = jnp.concatenate([before, block(s_ref, at + k, i, unroll + 2)], axis=0)
                c = block(c_ref, c_at + k, i + 1, unroll)
                p3 = 3.0 * p[1 : unroll + 2]
                flux = upwind(c, p[:unroll], p[1 : unroll + 1], p[2 : unroll + 2], p[3:], p3[:-1], p3[1:])
                west = jnp.concatenate([flux_before, flux[:-1]], axis=0)
                value = p[1 : unroll + 1] - (flux - west)
                if band is not None:
                    value = jnp.where(hits[k], moved[n * 3 + k], value)
                results.append((s_ref, at + k, i, value))
                after.append((flux[-1:], p[unroll : unroll + 1]))
        store(results)
        return tuple(after)

    carry = tuple(begin(at + k, c_at + k, first) for at, c_at, first in zonal for k in range(3))
    if count == 1:
        body(0, carry)
    else:
        lax.fori_loop(0, count, body, carry)


ZONAL_WIDE, ZONAL_MASKED, ZONAL_THIN, MERID_WIDE, MERID_THIN, C_SIZE = 0, 3, 6, 9, 12, 15


def spread_all(tab, band, wide, thin, out, base, zonal, merid, spans):
    for g, span, zonal_at, merid_at in ((wide, spans[0], ZONAL_WIDE, MERID_WIDE), (thin, spans[1], ZONAL_THIN, MERID_THIN)):
        scale, weight, cap = ([tab[band, kind, g, k] for k in range(3)] for kind in (2, 0, 3))
        masked = (base + ZONAL_MASKED, cap) if g is wide else ()
        spread(zonal[0], zonal[1] + g, out, base + zonal_at, scale, *span, *masked)
        spread(merid[0], merid[1] + g, out, base + merid_at, weight, *spans[2])


def keep(state_ref, s_ref, cycle, group):
    edge = 8 * cycle
    for k in range(3):
        i = group * 3 + k
        put_block(state_ref, cycle * 6 + i, 0, block(s_ref, i, edge, KEEP))
        put_block(state_ref, cycle * 6 + i, KEEP, block(s_ref, i, LON - edge - KEEP, KEEP))


def inner_kernel(tab, d_ref, cz_ref, cm_ref, s_ref, state_ref, step_ref, c_ref, r_ref):
    band = lax.axis_index("lat")
    is_cap = (band == 0) | (band == BANDS - 1)
    wide = jnp.where(band == BANDS - 1, 1, 0)
    thin = 1 - wide
    at_wide, at_thin = wide * 3, thin * 3
    inverse_wide, inverse_thin = ([tab[band, 1, g, k] for k in range(3)] for g in (wide, thin))
    spread_all(tab, band, wide, thin, c_ref, 0, (cz_ref, 0), (cm_ref, 0), ((0, LON // 8), (8, LON // 8 - 1), (8, LON // 8 - 2)))
    keep(state_ref, s_ref, 0, wide)
    keep(state_ref, s_ref, 0, thin)
    sweeps(s_ref, c_ref, r_ref, LON // 16, 16, [(at_wide, ZONAL_WIDE, 2)])

    for cycle in range(NSTEPS):
        edge = 8 * (cycle + 1)
        kept = LON - 2 * edge

        @pl.when(is_cap)
        def _(cycle=cycle):
            for sub in range(1, NSUB + 1):
                low = 2 * (NSUB * cycle + sub)
                if sub > 1:
                    width = LON - 2 * low
                    unroll = max(n for n in range(8, 31) if width % n == 0)
                    sweeps(s_ref, c_ref, r_ref, width // unroll, unroll, [(at_wide, ZONAL_MASKED, low)])
                if sub < NSUB:
                    for k in range(3):
                        at = (cycle * 3 + sub - 1) * 3 + k
                        put_block(step_ref, at, 0, block(s_ref, at_wide + k, low, 4))
                        put_block(step_ref, at, 4, block(s_ref, at_wide + k, LON - low - 4, 4))

        beside = band if cycle == 0 else None
        sweeps(s_ref, c_ref, r_ref, kept // 16, 16, [(at_thin, ZONAL_THIN, edge)], [(at_wide, MERID_WIDE, edge)], inverse_wide, beside)
        if cycle < NSTEPS - 1:
            keep(state_ref, s_ref, cycle + 1, wide)
            then = [(at_wide, ZONAL_WIDE, edge + 2)]
        else:
            then = []
        sweeps(s_ref, c_ref, r_ref, kept // 16, 16, then, [(at_thin, MERID_THIN, edge)], inverse_thin)
        if cycle < NSTEPS - 1:
            keep(state_ref, s_ref, cycle + 1, thin)


def run_inner(table, cells, cz, cm):
    shapes = [(6, INNER_COLS * 8, 128), (18, 2 * KEEP * 8, 128), (27, 64, 128)]
    scratch = [pltpu.VMEM((n, INNER_COLS * 8, 128), jnp.float32) for n in (C_SIZE, 6)]
    return vmem_call(inner_kernel, shapes, scratch, "inner_columns", {1: 0})(table, cells, cz, cm)


def outer_kernel(tab, cz_ref, cm_ref, rw_ref, re_ref, done_ref, state_ref, step_ref, out_hbm, s_ref, cu_ref, c_ref, w_ref, o_ref, out_sem):
    band = lax.axis_index("lat")
    is_cap = (band == 0) | (band == BANDS - 1)
    wide = jnp.where(band == BANDS - 1, 1, 0)
    thin = 1 - wide
    for g in range(2):
        for kind, own in ((0, cz_ref), (1, cm_ref)):
            put_block(cu_ref, kind * 2 + g, EDGE, block(own, g, 0, EDGE))
            put_block(cu_ref, 4 + kind * 2 + g, 0, block(own, g, LON - EDGE, EDGE))
    for side, recv in ((0, rw_ref), (1, re_ref)):
        at = 0
        plan = [(s_ref, side * 6 + wide * 3 + k, WIDE) for k in range(3)]
        plan += [(s_ref, side * 6 + thin * 3 + k, NARROW) for k in range(3)]
        plan += [(cu_ref, side * 4 + wide, WIDE_Z), (cu_ref, side * 4 + 2 + wide, WIDE_M)]
        plan += [(cu_ref, side * 4 + thin, NARROW_Z), (cu_ref, side * 4 + 2 + thin, NARROW_M)]
        for ref, index, width in plan:
            first = EDGE if side else EDGE - width
            put_block(ref, index, first, recv[at * 8 : (at + width) * 8, :].reshape(width, 8, 128))
            at += width

    def take(cycle, group):
        edge = 8 * cycle
        for k in range(3):
            i = group * 3 + k
            put_block(s_ref, i, EDGE + edge, block(state_ref, cycle * 6 + i, 0, KEEP))
            put_block(s_ref, 6 + i, EDGE - edge - KEEP, block(state_ref, cycle * 6 + i, KEEP, KEEP))

    def places(at, c_at, first):
        return [(side * 6 + at, side * C_SIZE + c_at, first[side]) for side in range(2)]

    def sweep(zonal, meridional=(), inverse=None, beside=None):
        sweeps(s_ref, c_ref, None, 2, 12, zonal, meridional, inverse, beside, ahead=False)

    def first_zonal(cycle):
        low = jnp.where(is_cap, 8 * cycle + 2, 8 * cycle + 8)
        return places(at_wide, ZONAL_WIDE, (EDGE - WIDE + low, EDGE - low))

    at_wide, at_thin = wide * 3, thin * 3
    inverse_wide, inverse_thin = ([tab[band, 1, g, k] for k in range(3)] for g in (wide, thin))
    for side in range(2):
        near = EDGE - WIDE + (0 if side else 8)
        spans = ((EDGE - WIDE, 6 if side else 7), (near, 6), (near, 5))
        spread_all(tab, band, wide, thin, c_ref, side * C_SIZE, (cu_ref, side * 4), (cu_ref, side * 4 + 2), spans)
    take(0, wide)
    take(0, thin)
    sweep(first_zonal(0))

    for cycle in range(NSTEPS):
        edge = 8 * (cycle + 1)
        first = (EDGE - WIDE + edge, EDGE - edge)

        @pl.when(is_cap)
        def _(cycle=cycle):
            for sub in range(1, NSUB + 1):
                low = 2 * (NSUB * cycle + sub)
                if sub > 1:
                    sweep(places(at_wide, ZONAL_MASKED, (EDGE - WIDE + low, EDGE - low)))
                if sub < NSUB:
                    for k in range(3):
                        at = (cycle * 3 + sub - 1) * 3 + k
                        put_block(s_ref, at_wide + k, EDGE + low, block(step_ref, at, 0, 4))
                        put_block(s_ref, 6 + at_wide + k, EDGE - low - 4, block(step_ref, at, 4, 4))

        beside = band if cycle == 0 else None
        sweep(places(at_thin, ZONAL_THIN, first), places(at_wide, MERID_WIDE, first), inverse_wide, beside)
        if cycle < NSTEPS - 1:
            take(cycle + 1, wide)
            then = first_zonal(cycle + 1)
        else:
            then = []
        sweep(then, places(at_thin, MERID_THIN, first), inverse_thin)
        if cycle < NSTEPS - 1:
            take(cycle + 1, thin)

    north = band == BANDS - 1
    shift = jnp.where(north, SHIFT_NORTH, SHIFT)

    def write_rows(tile, act):
        for is_this, shift_here in ((north, SHIFT_NORTH), (jnp.logical_not(north), SHIFT)):
            low = max(0, TILE_STEP * tile + 6 - shift_here)
            high = min(ROWS, TILE_STEP * (tile + 1) + 6 - shift_here)

            @pl.when(is_this)
            def _(low=low, high=high):
                for l in range(LEVELS):
                    rows = (high - low) * FIELDS
                    source = o_ref.at[l, pl.ds((8 + low) * FIELDS, rows), :]
                    act(pltpu.make_async_copy(source, out_hbm.at[l, pl.ds(low * FIELDS, rows), :], out_sem))

    for g in range(2):
        for side in range(2):
            tile = TILES[g][side]
            for k in range(3):
                for f in range(FIELDS):
                    at, row = g * 3 + k, 2 * f + side
                    west = s_ref[at, pl.ds(EDGE * 8 + row, WIDE, stride=8), :]
                    inner = done_ref[at, pl.ds(WIDE * 8 + row, LON - 2 * WIDE, stride=8), :]
                    east = s_ref[6 + at, pl.ds((EDGE - WIDE) * 8 + row, WIDE, stride=8), :]
                    w_ref[f] = jnp.concatenate([west, inner, east], axis=0).T
                    for l in range(LEVELS):
                        start = (8 + TILE_STEP * tile + 6 + k - shift) * FIELDS + f
                        o_ref[l, pl.ds(start, 38, stride=3 * FIELDS), :] = w_ref[f, pl.ds(CHUNKS * l + 2, 38), :]
            write_rows(tile, lambda copy: copy.start())
    for tile in range(4):
        write_rows(tile, lambda copy: copy.wait())


def run_outer(table, cz, cm, from_west, from_east, done, state, step):
    args = [pltpu.with_memory_space_constraint(x, pltpu.VMEM) for x in (table, cz, cm, from_west, from_east, done, state, step)]
    return pl.pallas_call(
        outer_kernel,
        out_shape=jax.ShapeDtypeStruct((LEVELS, ROWS * FIELDS, LON), jnp.float32),
        in_specs=[pl.BlockSpec(memory_space=pltpu.VMEM)] * len(args),
        out_specs=pl.BlockSpec(memory_space=pl.ANY),
        scratch_shapes=[
            pltpu.VMEM((12, 2 * EDGE * 8, 128), jnp.float32),
            pltpu.VMEM((8, 2 * EDGE * 8, 128), jnp.float32),
            pltpu.VMEM((2 * C_SIZE, 2 * EDGE * 8, 128), jnp.float32),
            pltpu.VMEM((FIELDS, 128, 128), jnp.float32),
            pltpu.VMEM((LEVELS, 472 * FIELDS, LON), jnp.float32),
            pltpu.SemaphoreType.DMA,
        ],
        compiler_params=pltpu.CompilerParams(vmem_limit_bytes=VMEM_BYTES),
        name="outer_columns",
    )(*args)


def shards(table, tracers, zonal, merid):
    tracers = tracers.transpose(1, 2, 0, 3).reshape(LEVELS, ROWS * FIELDS, LON)
    su, sv, zonal, merid = row_payload(tracers, zonal, merid)
    middle = pack_middle(tracers, zonal, merid, su)
    within, beyond = [], []
    for lon in range(LOOP):
        for band in range(BANDS):
            within.append((lon * BANDS + band, lon * BANDS + (band ^ 1)))
            if band in (0, BANDS - 1):
                target = (lon + LOOP // 2) % LOOP * BANDS + band
            else:
                target = lon * BANDS + (3 - band)
            beyond.append((lon * BANDS + band, target))
    ru = lax.ppermute(su, ("lon", "lat"), within)
    rv = lax.ppermute(sv, ("lon", "lat"), beyond)
    cells, cz, cm, to_west, to_east = pack_rims(middle, ru, rv)
    from_east = lax.ppermute(to_west, "lon", [(i, (i - 1) % LOOP) for i in range(LOOP)])
    from_west = lax.ppermute(to_east, "lon", [(i, (i + 1) % LOOP) for i in range(LOOP)])
    done, state, step = run_inner(table, cells, cz, cm)
    advected = run_outer(table, cz, cm, from_west, from_east, done, state, step)
    return advected.reshape(LEVELS, ROWS, FIELDS, LON).transpose(2, 0, 1, 3)


def solution(mesh):
    table = lane_tables()
    spec, out_spec = P("lev", "lat", "lon"), P(None, "lev", "lat", "lon")

    def run(tracers, zonal_courant, merid_courant):
        inner = functools.partial(shards, jnp.asarray(table))
        return jax.shard_map(inner, mesh=mesh, in_specs=(out_spec, spec, spec), out_specs=out_spec, check_vma=False)(
            tracers, zonal_courant, merid_courant
        )

    return run
```
